128 devices in a mesh: seq: 8 (over x_lo, z), shard: 16 (over x_hi, y, core).
Axes of the slice: x: 4 (x_hi: 2, x_lo: 2; x = x_hi * 2 + x_lo), y: 4, z: 4, core: 2. Of those that a mesh axis runs over, the one named last changes fastest.
Arguments:
- tokens: bfloat16 [16, 1024, 1024], P('shard', 'seq'), may hold values from -6 to 6
- attn_gain: bfloat16 [1024], P('shard'), may hold values from 0.5 to 1.5
- w_query: bfloat16 [1024, 1024], P('shard'), may hold values from -0.1875 to 0.1875
- w_key: bfloat16 [1024, 512], P('shard'), may hold values from -0.1875 to 0.1875
- w_value: bfloat16 [1024, 512], P('shard'), may hold values from -0.1875 to 0.1875
- q_gain: bfloat16 [64], P('shard'), may hold values from 1 to 2
- k_gain: bfloat16 [64], P('shard'), may hold values from 1 to 2
- w_out: bfloat16 [1024, 1024], P('shard'), may hold values from -0.5 to 0.5
- ffn_gain: bfloat16 [1024], P('shard'), may hold values from 0.5 to 1.5
- w_gate: bfloat16 [1024, 4608], P('shard'), may hold values from -0.1875 to 0.1875
- w_up: bfloat16 [1024, 4608], P('shard'), may hold values from -0.1875 to 0.1875
- w_down: bfloat16 [4608, 1024], P('shard'), may hold values from -0.1875 to 0.1875
- cotangent: bfloat16 [16, 1024, 1024], P('shard', 'seq'), may hold values from -6 to 6
Outputs:
- block_out: bfloat16 [16, 1024, 1024], P('shard', 'seq')
- grad_tokens: bfloat16 [16, 1024, 1024], P('shard', 'seq')
- grad_attn_gain: float32 [1024], P('shard')
- grad_w_query: float32 [1024, 1024], P('shard')
- grad_w_key: float32 [1024, 512], P('shard')
- grad_w_value: float32 [1024, 512], P('shard')
- grad_q_gain: float32 [64], P('shard')
- grad_k_gain: float32 [64], P('shard')
- grad_w_out: float32 [1024, 1024], P('shard')
- grad_ffn_gain: float32 [1024], P('shard')
- grad_w_gate: float32 [1024, 4608], P('shard')
- grad_w_up: float32 [1024, 4608], P('shard')
- grad_w_down: float32 [4608, 1024], P('shard')
The draws below stay inside these ranges and needn't reach their ends.
All inputs are finite; a program needn't handle non-finite values.
Results may differ from the reference program's by a relative error of at most 0.033.
Values may be sent and summed in bfloat16 or wider, within the bound.
No kernel may reach another device: no remote copies, remote signals or barrier semaphores. Data moves between devices by JAX's collectives and lax.ppermute only.
A program may use at most 192 MiB of HBM per device.

```python
import jax
import jax.numpy as jnp
from jax import lax

D = 1024
HEADS = 16
KV_HEADS = 8
HEAD_DIM = 64
FF = 4608
LENGTH = 1024
SEQS = 16


def level_of(stream_key, shape, shards, least, top_value):
    loudness = 1.0
    for axis_at, blocks in shards:
        heights = jax.random.uniform(jax.random.fold_in(jax.random.fold_in(stream_key, 6), axis_at), (blocks,), jnp.float32, least / len(shards), top_value / len(shards))
        loudness = loudness * jnp.repeat(jnp.exp(heights), shape[axis_at] // blocks).reshape((-1,) + (1,) * (len(shape) - 1 - axis_at))
    return loudness


def normal_values(rng, shape, deviation, bound, split=(), dtype=jnp.bfloat16):
    drawn = deviation * jax.random.normal(rng, shape, jnp.float32)
    if split:
        drawn = drawn * level_of(rng, shape, split, -0.22, 0.18)
    return jnp.clip(drawn, -bound, bound).astype(dtype)


def setup_inputs(seed: int = 0) -> dict:
    keys = jax.random.split(jax.random.key(seed), 14)
    return {
        "tokens": normal_values(keys[0], (SEQS, LENGTH, D), 1.0, 6.0, ((0, 16), (1, 8))),
        "attn_gain": jnp.clip(1.0 + 0.1 * jax.random.normal(keys[1], (D,), jnp.float32), 0.5, 1.5).astype(jnp.bfloat16),
        "w_query": normal_values(keys[2], (D, HEADS * HEAD_DIM), D ** -0.5, 0.1875, ((0, 16),)),
        "w_key": normal_values(keys[3], (D, KV_HEADS * HEAD_DIM), D ** -0.5, 0.1875, ((0, 16),)),
        "w_value": normal_values(keys[4], (D, KV_HEADS * HEAD_DIM), D ** -0.5, 0.1875, ((0, 16),)),
        "q_gain": jnp.clip(1.0 + 1.0 * jax.random.uniform(keys[5], (HEAD_DIM,), jnp.float32) ** level_of(keys[5], (HEAD_DIM,), ((0, 16),), -0.2, 0.2), 1.0, 2.0).astype(jnp.bfloat16),
        "k_gain": jnp.clip(1.0 + 1.0 * jax.random.uniform(keys[6], (HEAD_DIM,), jnp.float32) ** level_of(keys[6], (HEAD_DIM,), ((0, 16),), -0.2, 0.2), 1.0, 2.0).astype(jnp.bfloat16),
        "w_out": normal_values(keys[7], (HEADS * HEAD_DIM, D), (D // 8) ** -0.5, 0.5, ((0, 16),)),
        "ffn_gain": jnp.clip(1.0 + 0.1 * jax.random.normal(keys[8], (D,), jnp.float32), 0.5, 1.5).astype(jnp.bfloat16),
        "w_gate": normal_values(keys[9], (D, FF), D ** -0.5, 0.1875, ((0, 16),)),
        "w_up": normal_values(keys[10], (D, FF), D ** -0.5, 0.1875, ((0, 16),)),
        "w_down": normal_values(keys[11], (FF, D), (FF // 4) ** -0.5, 0.1875, ((0, 16),)),
        "cotangent": normal_values(keys[12], (SEQS, LENGTH, D), 1.0, 6.0, ((0, 16), (1, 8))),
    }


EPS = 1e-05
THETA = 1000000.0
HIGH = lax.Precision.HIGHEST

@jax.custom_vjp
def low(v):
    return lax.optimization_barrier(v.astype(jnp.bfloat16)).astype(jnp.float32)

@jax.custom_vjp
def low_back(v):
    return v

def low_keep(v):
    return (low(v), None)

def low_pass(kept, grad):
    return (grad,)

def back_keep(v):
    return (v, None)

def back_low(kept, grad):
    return (low(grad),)
low.defvjp(low_keep, low_pass)
low_back.defvjp(back_keep, back_low)

def rms_norm(values, weight):
    inverse = lax.rsqrt(lax.optimization_barrier(jnp.mean(values * values, axis=-1, keepdims=True)) + EPS)
    return values * inverse * weight

def rope_tables(positions):
    steps_half = jnp.arange(HEAD_DIM // 2).astype(jnp.float32)
    inverse = jnp.exp(-jnp.log(THETA) * 2.0 * steps_half / HEAD_DIM)
    angles = positions[:, None] * inverse[None, :]
    angles = jnp.concatenate([angles, angles], axis=-1)
    return (jnp.cos(angles), jnp.sin(angles))

def rotate(values, cosine_table, sine_table):
    midpoint = values.shape[-1] // 2
    turned = jnp.concatenate([-values[..., midpoint:], values[..., :midpoint]], axis=-1)
    return values * cosine_table[:, None, :] + turned * sine_table[:, None, :]

def layer(inputs, params):
    attn_scale, query_weight, key_weight, value_weight, q_scale, k_scale, out_weight, ffn_scale, gate_weight, up_weight, down_weight = params
    length = inputs.shape[0]
    groups = HEADS // KV_HEADS
    factor = HEAD_DIM ** (-0.5)
    cosine_table, sine_table = rope_tables(jnp.arange(length).astype(jnp.float32))
    normed = low(rms_norm(inputs, attn_scale))
    query_raw = low_back(jnp.dot(normed, query_weight, precision=HIGH)).reshape(length, HEADS, HEAD_DIM)
    key_raw = low_back(jnp.dot(normed, key_weight, precision=HIGH)).reshape(length, KV_HEADS, HEAD_DIM)
    values = low(low_back(jnp.dot(normed, value_weight, precision=HIGH))).reshape(length, KV_HEADS, HEAD_DIM)
    queries = low(low_back(rotate(rms_norm(query_raw, q_scale), cosine_table, sine_table)))
    key_rows = low(low_back(rotate(rms_norm(key_raw, k_scale), cosine_table, sine_table)))
    keys_wide = jnp.repeat(key_rows, groups, axis=1)
    values_wide = jnp.repeat(values, groups, axis=1)
    scores = low_back(jnp.einsum('qhd,khd->hqk', queries, keys_wide, precision=HIGH) * factor)
    allowed = jnp.arange(length)[None, :] <= jnp.arange(length)[:, None]
    scores = jnp.where(allowed[None], scores, -1e+30)
    weights_low = low(jax.nn.softmax(scores, axis=-1))
    attended = jnp.einsum('hqk,khd->qhd', weights_low, values_wide, precision=HIGH)
    attended = low(low_back(attended.reshape(length, HEADS * HEAD_DIM)))
    residual = inputs + low_back(jnp.dot(attended, out_weight, precision=HIGH))
    normed_ffn = low(rms_norm(residual, ffn_scale))
    gate_values = low_back(jnp.dot(normed_ffn, gate_weight, precision=HIGH))
    up_values = low_back(jnp.dot(normed_ffn, up_weight, precision=HIGH))
    hidden = low(jax.nn.silu(gate_values) * up_values)
    return residual + jnp.dot(hidden, down_weight, precision=HIGH)

def reference(tokens, attn_gain, w_query, w_key, w_value, q_gain, k_gain, w_out, ffn_gain, w_gate, w_up, w_down, cotangent):
    params = tuple((weight.astype(jnp.float32) for weight in (attn_gain, w_query, w_key, w_value, q_gain, k_gain, w_out, ffn_gain, w_gate, w_up, w_down)))

    def one_sequence(totals, inputs_pair):
        inputs, grad_out = inputs_pair
        output, pull_back = jax.vjp(layer, inputs.astype(jnp.float32), params)
        grad_inputs, grad_params = pull_back(grad_out.astype(jnp.float32))
        totals = tuple((running + adding for running, adding in zip(totals, grad_params)))
        return (totals, (output.astype(jnp.bfloat16), grad_inputs.astype(jnp.bfloat16)))
    zeros_start = tuple((jnp.zeros_like(weight) for weight in params))
    totals, (block_out, grad_tokens) = lax.scan(one_sequence, zeros_start, (tokens, cotangent))
    return (block_out, grad_tokens, totals[0], totals[1], totals[2], totals[3], totals[4], totals[5], totals[6], totals[7], totals[8], totals[9], totals[10])
```

```python
from functools import partial

import jax
import jax.numpy as jnp
from jax import lax
from jax.sharding import PartitionSpec as P

HEAD_DIM = 64


EPS = 1e-05
THETA = 1000000.0


def rms_norm(values, weight):
    inverse = lax.rsqrt(jnp.mean(values * values, axis=-1, keepdims=True) + EPS)
    return values * inverse * weight


def rope_tables(positions):
    steps_half = jnp.arange(HEAD_DIM // 2).astype(jnp.float32)
    inverse = jnp.exp(-jnp.log(THETA) * 2.0 * steps_half / HEAD_DIM)
    angles = positions[:, None] * inverse[None, :]
    angles = jnp.concatenate([angles, angles], axis=-1)
    return (jnp.cos(angles), jnp.sin(angles))


def rotate(values, cosine_table, sine_table):
    midpoint = values.shape[-1] // 2
    turned = jnp.concatenate([-values[..., midpoint:], values[..., :midpoint]], axis=-1)
    return values * cosine_table[:, None, :] + turned * sine_table[:, None, :]


def qk_local(query_raw, key_raw, q_scale, k_scale, cosine_table, sine_table):
    row_count = query_raw.shape[0]
    queries = rotate(
        rms_norm(query_raw.reshape(row_count, -1, HEAD_DIM), q_scale), cosine_table, sine_table
    )
    key_rows = rotate(
        rms_norm(key_raw.reshape(row_count, -1, HEAD_DIM), k_scale), cosine_table, sine_table
    )
    return (queries.reshape(row_count, -1), key_rows.reshape(row_count, -1))


def swiglu(gate_values, up_values):
    return jax.nn.silu(gate_values) * up_values


def block_scores(query_block, key_heads, first_row, factor):
    block_rows = query_block.shape[0]
    length = key_heads.shape[0]
    scores = (
        jnp.einsum("qkgd,tkd->kgqt", query_block, key_heads, preferred_element_type=jnp.float32)
        * factor
    )
    query_index = first_row + jnp.arange(block_rows, dtype=jnp.int32)
    allowed = jnp.arange(length, dtype=jnp.int32)[None, :] <= query_index[:, None]
    return jnp.where(allowed, scores, -1e30)


def attend(query_heads, key_heads, value_heads):
    length = key_heads.shape[0]
    block_rows = min(512, length)
    block_count = length // block_rows
    factor = HEAD_DIM ** (-0.5)
    blocks = query_heads.reshape((block_count, block_rows) + query_heads.shape[1:])
    starts = jnp.arange(block_count, dtype=jnp.int32) * block_rows

    def one_block(block_item):
        query_block, first_row = block_item
        scores = block_scores(query_block, key_heads, first_row, factor)
        row_max = jnp.max(scores, axis=-1, keepdims=True)
        exponent = jnp.exp(scores - row_max)
        row_sum = jnp.sum(exponent, axis=-1, keepdims=True)
        weights_low = (exponent / row_sum).astype(jnp.bfloat16)
        output = jnp.einsum(
            "kgqt,tkd->qkgd", weights_low, value_heads, preferred_element_type=jnp.float32
        )
        return (output.astype(jnp.bfloat16), (row_max + jnp.log(row_sum))[..., 0])

    outputs, log_totals = lax.map(one_block, (blocks, starts))
    return (outputs.reshape(length, -1), log_totals)


def attend_back(query_heads, key_heads, value_heads, grad_heads, log_totals):
    length = key_heads.shape[0]
    block_rows = min(512, length)
    block_count = length // block_rows
    factor = HEAD_DIM ** (-0.5)
    query_blocks = query_heads.reshape((block_count, block_rows) + query_heads.shape[1:])
    grad_blocks = grad_heads.reshape((block_count, block_rows) + grad_heads.shape[1:])
    starts = jnp.arange(block_count, dtype=jnp.int32) * block_rows

    def one_block(running, block_item):
        key_total, value_total = running
        query_block, grad_block, lse_block, first_row = block_item
        scores = block_scores(query_block, key_heads, first_row, factor)
        exact = jnp.exp(scores - lse_block[..., None])
        grad_weights = jnp.einsum(
            "qkgd,tkd->kgqt", grad_block, value_heads, preferred_element_type=jnp.float32
        )
        inner_sum = jnp.sum(exact * grad_weights, axis=-1, keepdims=True)
        grad_scores = (exact * (grad_weights - inner_sum)).astype(jnp.bfloat16)
        grad_query = (
            jnp.einsum("kgqt,tkd->qkgd", grad_scores, key_heads, preferred_element_type=jnp.float32)
            * factor
        )
        key_total = (
            key_total
            + jnp.einsum(
                "kgqt,qkgd->tkd", grad_scores, query_block, preferred_element_type=jnp.float32
            )
            * factor
        )
        value_total = value_total + jnp.einsum(
            "kgqt,qkgd->tkd",
            exact.astype(jnp.bfloat16),
            grad_block,
            preferred_element_type=jnp.float32,
        )
        return ((key_total, value_total), grad_query)

    empty = jnp.zeros(key_heads.shape, jnp.float32)
    (grad_keys, grad_values), grad_queries = lax.scan(
        one_block, (empty, empty), (query_blocks, grad_blocks, log_totals, starts)
    )
    return (grad_queries.reshape(length, -1), grad_keys, grad_values)


def y_perm(step):
    return [
        (half * 8 + ((y + step) % 4) * 2 + core, half * 8 + y * 2 + core)
        for half in range(2)
        for y in range(4)
        for core in range(2)
    ]


CORE_SWAP = [(index, index ^ 1) for index in range(16)]
HALF_SWAP = [(index, index ^ 8) for index in range(16)]
GROUPS = [list(range(8)), list(range(8, 16))]


def gather_group(block):
    ring = jnp.stack([block] + [lax.ppermute(block, "shard", y_perm(step)) for step in (1, 2, 3)])
    return jnp.concatenate([ring, lax.ppermute(ring, "shard", CORE_SWAP)])


def scatter_group(parts):
    other = lax.ppermute(parts[4:].astype(jnp.bfloat16), "shard", CORE_SWAP)
    ring = parts[:4] + other.astype(jnp.float32)
    total = ring[0]
    for step in (1, 2, 3):
        arrived = lax.ppermute(ring[step].astype(jnp.bfloat16), "shard", y_perm(4 - step))
        total = total + arrived.astype(jnp.float32)
    return total


def both_halves(block, half):
    other = lax.ppermute(block, "shard", HALF_SWAP)
    first = half == 0
    return jnp.stack([jnp.where(first, block, other), jnp.where(first, other, block)])


def dot(left, right, contract):
    return lax.dot_general(left, right, (contract, ((), ())), preferred_element_type=jnp.float32)


def per_device(
    tokens,
    attn_gain,
    w_query,
    w_key,
    w_value,
    q_gain,
    k_gain,
    w_out,
    ffn_gain,
    w_gate,
    w_up,
    w_down,
    cotangent,
):
    low = jnp.bfloat16
    shard = lax.axis_index("shard")
    half, core = shard // 8, shard % 2
    own_tokens = tokens[0]
    rows, width = own_tokens.shape
    seq_parts = lax.axis_size("seq")

    gains = jnp.concatenate([attn_gain, ffn_gain, q_gain, k_gain])
    gain_row = jnp.pad(gains, (0, 1408 - gains.shape[0]))
    columns = jnp.concatenate(
        [
            w_query.reshape(64, 2, 4, 128).transpose(2, 1, 0, 3).reshape(8, 64, 128),
            w_key.reshape(64, 2, 4, 64).transpose(2, 1, 0, 3).reshape(8, 64, 64),
            w_value.reshape(64, 2, 4, 64).transpose(2, 1, 0, 3).reshape(8, 64, 64),
            w_gate.reshape(64, 2, 8, 288).transpose(2, 0, 1, 3).reshape(8, 64, 576),
            w_up.reshape(64, 2, 8, 288).transpose(2, 0, 1, 3).reshape(8, 64, 576),
        ],
        axis=2,
    )
    columns = jnp.concatenate(
        [columns, jnp.broadcast_to(gain_row[None, None], (8, 8, 1408))], axis=1
    )
    columns = lax.all_to_all(
        columns, "shard", 0, 0, axis_index_groups=GROUPS, tiled=True
    )
    halves_qkv = both_halves(columns[:, :, :256], half)
    halves_ffn = both_halves(columns[:, :64, 256:], half)
    gain_all = halves_qkv[:, :, 64, :136].reshape(16, 136).astype(jnp.float32)
    attn_scale = gain_all[:, :64].reshape(-1)
    ffn_scale = gain_all[:, 64:128].reshape(-1)
    q_scale = gain_all[:, 128:132].reshape(-1)
    k_scale = gain_all[:, 132:136].reshape(-1)
    weight_qkv = halves_qkv[:, :, :64].reshape(width, 256)
    weight_gate = halves_ffn[..., :576].reshape(width, 576)
    weight_up = halves_ffn[..., 576:].reshape(width, 576)
    weight_down = both_halves(w_down, half).reshape(576, width)
    out_halves = both_halves(w_out, half)
    out_own = jnp.where(core == 0, out_halves[0], out_halves[1])
    out_other = lax.ppermute(
        jnp.where(core == 0, out_halves[1], out_halves[0]), "shard", CORE_SWAP
    )
    weight_out = jnp.concatenate(
        [jnp.where(core == 0, out_own, out_other), jnp.where(core == 0, out_other, out_own)]
    )

    group_tokens = gather_group(own_tokens).reshape(-1, width)
    group_cotangent = gather_group(cotangent[0]).reshape(-1, width)

    positions = (lax.axis_index("seq") * rows + jnp.arange(rows, dtype=jnp.int32)).astype(
        jnp.float32
    )
    cosine_table, sine_table = (jnp.tile(table, (8, 1)) for table in rope_tables(positions))
    rope_local = partial(qk_local, cosine_table=cosine_table, sine_table=sine_table)
    normed = rms_norm(group_tokens.astype(jnp.float32), attn_scale).astype(low)
    raw = dot(normed, weight_qkv, ((1,), (0,)))
    query_raw, key_raw, value_raw = raw[:, :128], raw[:, 128:192], raw[:, 192:]
    query_rot, key_rot = rope_local(query_raw, key_raw, q_scale, k_scale)
    heads = jnp.concatenate([query_rot, key_rot, value_raw], axis=1).astype(low)
    heads = lax.all_to_all(heads, "seq", 0, 0, tiled=True)
    length = heads.shape[0]
    query_heads = heads[:, :128].reshape(length, 1, 2, HEAD_DIM)
    key_heads = heads[:, 128:192].reshape(length, 1, HEAD_DIM)
    value_heads = heads[:, 192:].reshape(length, 1, HEAD_DIM)
    attended, log_totals = attend(query_heads, key_heads, value_heads)
    attended = lax.all_to_all(attended, "seq", 0, 0, tiled=True)

    inputs = own_tokens.astype(jnp.float32)
    mixed = dot(attended, weight_out, ((1,), (0,))).reshape(8, rows, width)
    residual = inputs + scatter_group(mixed)
    normed_own = rms_norm(residual, ffn_scale).astype(low)
    normed_ffn = gather_group(normed_own).reshape(-1, width)
    gate_values = dot(normed_ffn, weight_gate, ((1,), (0,)))
    up_values = dot(normed_ffn, weight_up, ((1,), (0,)))
    hidden = swiglu(gate_values, up_values).astype(low)
    down = dot(hidden, weight_down, ((1,), (0,))).reshape(8, rows, width)
    block_out = (residual + scatter_group(down)).astype(low)[None]

    grad_w_down = dot(hidden, group_cotangent, ((0,), (0,)))
    grad_hidden = dot(group_cotangent, weight_down, ((1,), (1,)))
    _, swiglu_pull = jax.vjp(swiglu, gate_values, up_values)
    grad_gate, grad_up = swiglu_pull(grad_hidden)
    grad_gate, grad_up = grad_gate.astype(low), grad_up.astype(low)
    grad_w_gate = dot(normed_ffn, grad_gate, ((0,), (0,)))
    grad_w_up = dot(normed_ffn, grad_up, ((0,), (0,)))
    grad_normed_ffn = dot(grad_gate, weight_gate, ((1,), (1,))) + dot(
        grad_up, weight_up, ((1,), (1,))
    )
    grad_normed_ffn = scatter_group(grad_normed_ffn.reshape(8, rows, width))
    _, ffn_pull = jax.vjp(rms_norm, residual, ffn_scale)
    grad_residual, grad_ffn_gain = ffn_pull(grad_normed_ffn)
    grad_residual = grad_residual + cotangent[0].astype(jnp.float32)
    grad_branch = gather_group(grad_residual.astype(low)).reshape(-1, width)
    grad_w_out = dot(attended, grad_branch, ((0,), (0,)))
    grad_attended = dot(grad_branch, weight_out, ((1,), (1,))).astype(low)
    grad_heads = lax.all_to_all(grad_attended, "seq", 0, 0, tiled=True)
    grad_queries, grad_keys, grad_values = attend_back(
        query_heads, key_heads, value_heads, grad_heads.reshape(length, 1, 2, HEAD_DIM), log_totals
    )
    back = jnp.concatenate([grad_queries, grad_keys[:, 0], grad_values[:, 0]], axis=1).astype(low)
    back = lax.all_to_all(back, "seq", 0, 0, tiled=True)
    _, rope_pull = jax.vjp(rope_local, query_raw, key_raw, q_scale, k_scale)
    grad_query_raw, grad_key_raw, grad_q_gain, grad_k_gain = rope_pull(
        (back[:, :128].astype(jnp.float32), back[:, 128:192].astype(jnp.float32))
    )
    grad_raw = jnp.concatenate(
        [grad_query_raw.astype(low), grad_key_raw.astype(low), back[:, 192:]], axis=1
    )
    grad_w_qkv = dot(normed, grad_raw, ((0,), (0,)))
    grad_normed = scatter_group(
        dot(grad_raw, weight_qkv, ((1,), (1,))).reshape(8, rows, width)
    )
    _, attn_pull = jax.vjp(rms_norm, inputs, attn_scale)
    grad_inputs, grad_attn_gain = attn_pull(grad_normed)
    grad_tokens = (grad_inputs + grad_residual).astype(low)[None]

    grad_gains = jnp.concatenate(
        [
            grad_attn_gain.reshape(16, 64),
            grad_ffn_gain.reshape(16, 64),
            grad_q_gain.reshape(16, 4),
            grad_k_gain.reshape(16, 4),
        ],
        axis=1,
    ).astype(low)
    grad_gains = jnp.broadcast_to(
        jnp.pad(grad_gains, ((0, 0), (0, 1408 - 136)))[:, None, None], (16, 8, 1, 1408)
    )
    grad_columns = jnp.concatenate([grad_w_qkv, grad_w_gate, grad_w_up], axis=1).astype(low)
    grad_columns = jnp.concatenate([grad_columns.reshape(16, 8, 8, 1408), grad_gains], axis=2)
    grad_columns = grad_columns.transpose(1, 0, 2, 3).reshape(128, 9, 1408)
    grad_columns = lax.all_to_all(grad_columns, ("seq", "shard"), 0, 0, tiled=True)
    grad_columns = (
        grad_columns.reshape(8, 2, 8, 9, 1408).astype(jnp.float32).sum((0, 1))
    )
    gain_sums = grad_columns[:, 8, :136].sum(0)

    grad_rows = jnp.concatenate(
        [
            grad_w_down.reshape(2, 8, 36, width).transpose(1, 0, 2, 3),
            grad_w_out.reshape(2, 8, 8, width).transpose(1, 0, 2, 3),
        ],
        axis=2,
    ).astype(low)
    grad_rows = lax.all_to_all(grad_rows, "seq", 0, 0, tiled=True)
    grad_rows = grad_rows.astype(jnp.float32).sum(0)
    down_rows, out_rows = grad_rows[:, :36].astype(low), grad_rows[:, 36:].astype(low)
    down_keep = jnp.where(half == 0, grad_rows[0, :36], grad_rows[1, :36])
    down_send = jnp.where(half == 0, down_rows[1], down_rows[0])
    out_keep = jnp.where(core == 0, grad_rows[0, 36:], grad_rows[1, 36:])
    out_send = jnp.where(core == 0, out_rows[1], out_rows[0])
    out_arrived = lax.ppermute(out_send, "shard", CORE_SWAP).astype(jnp.float32)
    first, second = (
        jnp.where(core == 0, out_keep, out_arrived),
        jnp.where(core == 0, out_arrived, out_keep),
    )
    out_mine = jnp.where(half == 0, first, second)
    out_theirs = jnp.where(half == 0, second, first)
    rows_arrived = lax.ppermute(
        jnp.concatenate([down_send, out_theirs.astype(low)]), "shard", HALF_SWAP
    ).astype(jnp.float32)
    row_sums = jnp.concatenate([down_keep, out_mine]) + rows_arrived

    shares = jnp.concatenate(
        [grad_columns[:, :8].reshape(-1).astype(low), row_sums.reshape(-1).astype(low)]
    ).reshape(1, -1, 128)
    shares = lax.all_to_all(
        jnp.broadcast_to(shares, (8,) + shares.shape[1:]), "seq", 0, 0, tiled=True
    ).reshape(8, -1)
    columns_all = shares[:, : 8 * 8 * 1408].reshape(8, 8, 8, 1408).astype(jnp.float32)
    rows_all = shares[:, 8 * 8 * 1408 :].reshape(8, 44, width).astype(jnp.float32)

    def by_head(part):
        size = part.shape[-1]
        part = part.reshape(8, 4, 2, 8, size).transpose(0, 3, 2, 1, 4)
        return part.reshape(64, 8 * size)

    def by_half(part):
        part = part.reshape(8, 8, 8, 2, 288).transpose(0, 2, 3, 1, 4)
        return part.reshape(64, 4608)

    return (
        block_out,
        grad_tokens,
        gain_sums[:64],
        by_head(columns_all[..., :128]),
        by_head(columns_all[..., 128:192]),
        by_head(columns_all[..., 192:256]),
        gain_sums[128:132],
        gain_sums[132:136],
        rows_all[:, 36:].reshape(64, width),
        gain_sums[64:128],
        by_half(columns_all[..., 256:832]),
        by_half(columns_all[..., 832:]),
        rows_all[:, :36].reshape(288, width),
    )


def solution(mesh):
    placed = (
        P("shard", "seq", None),
        P("shard"),
        P("shard", None),
        P("shard", None),
        P("shard", None),
        P("shard"),
        P("shard"),
        P("shard", None),
        P("shard"),
        P("shard", None),
        P("shard", None),
        P("shard", None),
        P("shard", "seq", None),
    )
    return jax.shard_map(
        per_device,
        mesh=mesh,
        in_specs=placed,
        out_specs=(
            P("shard", "seq", None),
            P("shard", "seq", None),
            P("shard"),
            P("shard", None),
            P("shard", None),
            P("shard", None),
            P("shard"),
            P("shard"),
            P("shard", None),
            P("shard"),
            P("shard", None),
            P("shard", None),
            P("shard", None),
        ),
        check_vma=False,
    )
```

```python
from functools import partial

import jax
import jax.numpy as jnp
from jax import lax
from jax.experimental import pallas as pl
from jax.experimental.pallas import tpu as pltpu
from jax.sharding import PartitionSpec as P

HEAD_DIM = 64


EPS = 1e-05
THETA = 1000000.0


def rms_norm(values, weight):
    inverse = lax.rsqrt(jnp.mean(values * values, axis=-1, keepdims=True) + EPS)
    return values * inverse * weight


def rope_tables(positions):
    steps_half = jnp.arange(HEAD_DIM // 2).astype(jnp.float32)
    inverse = jnp.exp(-jnp.log(THETA) * 2.0 * steps_half / HEAD_DIM)
    angles = positions[:, None] * inverse[None, :]
    angles = jnp.concatenate([angles, angles], axis=-1)
    return (jnp.cos(angles), jnp.sin(angles))


def rotate(values, cosine_table, sine_table):
    midpoint = values.shape[-1] // 2
    turned = jnp.concatenate([-values[..., midpoint:], values[..., :midpoint]], axis=-1)
    return values * cosine_table[:, None, :] + turned * sine_table[:, None, :]


def qk_local(query_raw, key_raw, q_scale, k_scale, cosine_table, sine_table):
    row_count = query_raw.shape[0]
    queries = rotate(
        rms_norm(query_raw.reshape(row_count, -1, HEAD_DIM), q_scale), cosine_table, sine_table
    )
    key_rows = rotate(
        rms_norm(key_raw.reshape(row_count, -1, HEAD_DIM), k_scale), cosine_table, sine_table
    )
    return (queries.reshape(row_count, -1), key_rows.reshape(row_count, -1))


def swiglu(gate_values, up_values):
    return jax.nn.silu(gate_values) * up_values


def dot(left, right, contract):
    return lax.dot_general(left, right, (contract, ((), ())), preferred_element_type=jnp.float32)


BLOCK = 256


def scores_block(query, keys, first):
    scores = dot(keys, query, ((1,), (1,)))
    key_index = lax.broadcasted_iota(jnp.int32, scores.shape, 0)
    query_index = first + lax.broadcasted_iota(jnp.int32, scores.shape, 1)
    return jnp.where(key_index <= query_index, scores, -1e30)


def attend_kernel(heads_ref, out_ref, lse_ref):
    length = heads_ref.shape[0]
    values_turned = heads_ref[:, 192:].T
    for first in range(0, length, BLOCK):
        end = first + BLOCK
        keys = heads_ref[:end, 128:192]
        parts = []
        for head in range(2):
            query = heads_ref[first:end, head * HEAD_DIM : (head + 1) * HEAD_DIM] * 0.125
            scores = scores_block(query, keys, first)
            row_max = jnp.max(scores, axis=0, keepdims=True)
            exponent = jnp.exp(scores - row_max)
            row_sum = jnp.sum(exponent, axis=0, keepdims=True)
            parts.append(
                dot(values_turned[:, :end], exponent.astype(jnp.bfloat16), ((1,), (0,))) / row_sum
            )
            lse_ref[head : head + 1, first:end] = row_max + jnp.log(row_sum)
        out_ref[first:end, :] = jnp.concatenate(parts).T.astype(jnp.bfloat16)


def attend_back_kernel(heads_ref, grad_ref, lse_ref, out_ref, keys_total, values_total):
    length = heads_ref.shape[0]
    keys_turned = heads_ref[:, 128:192].T
    keys_total[...] = jnp.zeros_like(keys_total)
    values_total[...] = jnp.zeros_like(values_total)
    for first in range(0, length, BLOCK):
        end = first + BLOCK
        keys = heads_ref[:end, 128:192]
        values = heads_ref[:end, 192:]
        parts = []
        for head in range(2):
            lanes = slice(head * HEAD_DIM, (head + 1) * HEAD_DIM)
            query = heads_ref[first:end, lanes] * 0.125
            grad = grad_ref[first:end, lanes]
            exact = jnp.exp(
                scores_block(query, keys, first) - lse_ref[head : head + 1, first:end]
            )
            grad_probs = dot(values, grad, ((1,), (1,)))
            inner = jnp.sum(exact * grad_probs, axis=0, keepdims=True)
            grad_scores = (exact * (grad_probs - inner)).astype(jnp.bfloat16)
            parts.append(dot(keys_turned[:, :end], grad_scores, ((1,), (0,))) * 0.125)
            keys_total[:end, :] += dot(grad_scores, query, ((1,), (0,)))
            values_total[:end, :] += dot(exact.astype(jnp.bfloat16), grad, ((1,), (0,)))
        out_ref[first:end, :128] = jnp.concatenate(parts).T.astype(jnp.bfloat16)
    out_ref[:, 128:] = jnp.concatenate([keys_total[...], values_total[...]], axis=1).astype(
        jnp.bfloat16
    )


VMEM = pl.BlockSpec(memory_space=pltpu.VMEM)


def attend(heads):
    length = heads.shape[0]
    return pl.pallas_call(
        attend_kernel,
        out_shape=(
            jax.ShapeDtypeStruct((length, 128), jnp.bfloat16),
            jax.ShapeDtypeStruct((2, length), jnp.float32),
        ),
        in_specs=[VMEM],
        out_specs=(VMEM, VMEM),
        compiler_params=pltpu.CompilerParams(vmem_limit_bytes=32 * 2**20),
        cost_estimate=pl.CostEstimate(
            flops=5 * 10**8, bytes_accessed=2**20, transcendentals=2 * length * length
        ),
    )(heads)


def attend_back(heads, grad_heads, log_totals):
    length = heads.shape[0]
    return pl.pallas_call(
        attend_back_kernel,
        out_shape=jax.ShapeDtypeStruct((length, 256), jnp.bfloat16),
        in_specs=[VMEM] * 3,
        out_specs=VMEM,
        scratch_shapes=[pltpu.VMEM((length, HEAD_DIM), jnp.float32)] * 2,
        compiler_params=pltpu.CompilerParams(vmem_limit_bytes=32 * 2**20),
        cost_estimate=pl.CostEstimate(
            flops=10**9, bytes_accessed=2**20, transcendentals=2 * length * length
        ),
    )(heads, grad_heads, log_totals)


def call(kernel, out_shape, *operands, flops=10**6):
    several = isinstance(out_shape, tuple)
    return pl.pallas_call(
        kernel,
        out_shape=out_shape,
        in_specs=[VMEM] * len(operands),
        out_specs=(VMEM,) * len(out_shape) if several else VMEM,
        compiler_params=pltpu.CompilerParams(vmem_limit_bytes=48 * 2**20),
        cost_estimate=pl.CostEstimate(flops=flops, bytes_accessed=2**20, transcendentals=0),
    )(*operands)


def stack_kernel(*refs):
    *pieces, out_ref = refs
    row = 0
    for piece in pieces:
        out_ref[row : row + piece.shape[0], :] = piece[...]
        row += piece.shape[0]


def stack_rows(*pieces):
    rows = sum(piece.shape[0] for piece in pieces)
    return call(
        stack_kernel, jax.ShapeDtypeStruct((rows, pieces[0].shape[1]), pieces[0].dtype), *pieces
    )


def head_index(place):
    return place % 2 * 4 + place // 2


def pack_heads_kernel(query_ref, key_ref, value_ref, gain_ref, out_ref):
    for place in range(8):
        head = head_index(place)
        narrow = slice(head * HEAD_DIM, (head + 1) * HEAD_DIM)
        block = jnp.concatenate(
            [
                query_ref[:, head * 128 : (head + 1) * 128],
                key_ref[:, narrow],
                value_ref[:, narrow],
            ],
            axis=1,
        )
        for half in range(2):
            out_ref[half * 8 + place, :64, :] = block
            out_ref[half * 8 + place, 64:, :] = gain_ref[...]


def pack_ffn_kernel(gate_ref, up_ref, out_ref):
    for place in range(8):
        low, high = place * 288, (8 + place) * 288
        out_ref[place] = jnp.concatenate(
            [
                gate_ref[:, low : low + 288],
                gate_ref[:, high : high + 288],
                up_ref[:, low : low + 288],
                up_ref[:, high : high + 288],
            ],
            axis=1,
        )


def unpack_ffn_kernel(share_ref, gate_ref, up_ref, down_ref, out_ref):
    for place in range(8):
        block = share_ref[:, place * 8 : place * 8 + 8, :].astype(jnp.float32).reshape(64, 1152)
        low, high = place * 288, (8 + place) * 288
        gate_ref[:, low : low + 288] = block[:, :288]
        gate_ref[:, high : high + 288] = block[:, 288:576]
        up_ref[:, low : low + 288] = block[:, 576:864]
        up_ref[:, high : high + 288] = block[:, 864:]
    for part in range(8):
        lanes = slice(part * 128, (part + 1) * 128)
        for piece in range(9):
            down_ref[piece * 32 : (piece + 1) * 32, lanes] = share_ref[
                part, 64:96, piece * 128 : (piece + 1) * 128
            ].astype(jnp.float32)
        for piece in range(8):
            out_ref[piece * 8 : (piece + 1) * 8, lanes] = share_ref[
                part, 96:104, piece * 128 : (piece + 1) * 128
            ].astype(jnp.float32)


def unpack_heads_kernel(share_ref, query_ref, key_ref, value_ref):
    for place in range(8):
        head = head_index(place)
        block = share_ref[:, place * 8 : place * 8 + 8, :].astype(jnp.float32).reshape(64, 256)
        query_ref[:, head * 128 : (head + 1) * 128] = block[:, :128]
        key_ref[:, head * HEAD_DIM : (head + 1) * HEAD_DIM] = block[:, 128:192]
        value_ref[:, head * HEAD_DIM : (head + 1) * HEAD_DIM] = block[:, 192:]


def near_kernel(turned, left_ref, right_ref, far_ref, own_ref, *send_refs):
    rows = own_ref.shape[0]
    total = dot(left_ref[:512, :], right_ref[...], ((1,), (1 if turned else 0,)))
    total = total + far_ref[...].astype(jnp.float32)
    own_ref[...] = total[:rows]
    for step, send_ref in enumerate(send_refs, 1):
        send_ref[...] = total[step * rows : (step + 1) * rows].astype(jnp.bfloat16)


def y_perm(step):
    return [
        (half * 8 + ((y + step) % 4) * 2 + core, half * 8 + y * 2 + core)
        for half in range(2)
        for y in range(4)
        for core in range(2)
    ]


CORE_SWAP = [(index, index ^ 1) for index in range(16)]
HALF_SWAP = [(index, index ^ 8) for index in range(16)]
GROUPS = [list(range(8)), list(range(8, 16))]


def swap_cores(block):
    return lax.ppermute(block, "shard", CORE_SWAP)


def gather_group(block):
    near = [block] + [lax.ppermute(block, "shard", y_perm(step)) for step in (1, 2, 3)]
    return stack_rows(*near, *[swap_cores(piece) for piece in near])


def multiply_scatter(left, right, turned):
    far = dot(left[512:], right, ((1,), (1 if turned else 0,)))
    far = swap_cores(far.astype(jnp.bfloat16))
    width = far.shape[1]
    wide, low = (
        jax.ShapeDtypeStruct((128, width), dtype) for dtype in (jnp.float32, jnp.bfloat16)
    )
    total, *sends = call(
        partial(near_kernel, turned),
        (wide, low, low, low),
        left,
        right,
        far,
        flops=2 * 512 * left.shape[1] * width,
    )
    for step, send in enumerate(sends, 1):
        arrived = lax.ppermute(send, "shard", y_perm(4 - step))
        total = total + arrived.astype(jnp.float32)
    return total


def both_halves(block, half):
    other = lax.ppermute(block, "shard", HALF_SWAP)
    first = half == 0
    return jnp.stack([jnp.where(first, block, other), jnp.where(first, other, block)])


def tie(*arrays):
    return lax.optimization_barrier(arrays)


def per_device(
    tokens,
    attn_gain,
    w_query,
    w_key,
    w_value,
    q_gain,
    k_gain,
    w_out,
    ffn_gain,
    w_gate,
    w_up,
    w_down,
    cotangent,
):
    low, wide = jnp.bfloat16, jnp.float32
    shard = lax.axis_index("shard")
    half, core = shard // 8, shard % 2
    own_tokens = tokens[0]
    rows, width = own_tokens.shape
    group_tokens = gather_group(own_tokens)

    gains = jnp.concatenate([attn_gain, ffn_gain, q_gain, k_gain])
    gain_rows = jnp.broadcast_to(jnp.pad(gains, (0, 120))[None], (16, 256))
    head_columns = call(
        pack_heads_kernel,
        jax.ShapeDtypeStruct((16, 80, 256), low),
        w_query,
        w_key,
        w_value,
        gain_rows,
    )
    head_columns = lax.all_to_all(head_columns, "shard", 0, 0, tiled=True)
    gain_all = head_columns[:, 64, :136].astype(wide)
    attn_scale = gain_all[:, :64].reshape(-1)
    ffn_scale = gain_all[:, 64:128].reshape(-1)
    q_scale = gain_all[:, 128:132].reshape(-1)
    k_scale = gain_all[:, 132:136].reshape(-1)
    weight_qkv = head_columns[:, :64].reshape(width, 256)

    positions = (lax.axis_index("seq") * rows + jnp.arange(rows, dtype=jnp.int32)).astype(wide)
    cosine_table, sine_table = (jnp.tile(table, (8, 1)) for table in rope_tables(positions))
    rope_local = partial(qk_local, cosine_table=cosine_table, sine_table=sine_table)
    wide_tokens = group_tokens.astype(wide)
    scaled = wide_tokens * lax.rsqrt(
        jnp.mean(wide_tokens * wide_tokens, axis=-1, keepdims=True) + EPS
    )
    normed = (scaled * attn_scale).astype(low)
    raw = dot(normed, weight_qkv, ((1,), (0,)))
    query_raw, key_raw, value_raw = raw[:, :128], raw[:, 128:192], raw[:, 192:]
    query_rot, key_rot = rope_local(query_raw, key_raw, q_scale, k_scale)
    heads = jnp.concatenate([query_rot, key_rot, value_raw], axis=1).astype(low)

    ffn_columns = call(
        pack_ffn_kernel, jax.ShapeDtypeStruct((8, 64, 1152), low), w_gate, w_up
    )
    ffn_columns = lax.all_to_all(
        ffn_columns, "shard", 0, 0, axis_index_groups=GROUPS, tiled=True
    )
    weight_down = both_halves(w_down, half).reshape(576, width)
    out_halves = both_halves(w_out, half)
    out_own = jnp.where(core == 0, out_halves[0], out_halves[1])
    out_other = swap_cores(jnp.where(core == 0, out_halves[1], out_halves[0]))
    weight_out = jnp.concatenate(
        [jnp.where(core == 0, out_own, out_other), jnp.where(core == 0, out_other, out_own)]
    )

    heads = lax.all_to_all(heads, "seq", 0, 0, tiled=True)
    attended, log_totals = attend(heads)
    attended, ffn_columns, weight_down, weight_out = tie(
        attended, ffn_columns, weight_down, weight_out
    )
    weight_ffn = both_halves(ffn_columns, half).reshape(width, 1152)
    group_cotangent = gather_group(cotangent[0])
    attended = lax.all_to_all(attended, "seq", 0, 0, tiled=True)
    attended, group_cotangent = tie(attended, group_cotangent)

    inputs = own_tokens.astype(wide)
    residual = inputs + multiply_scatter(attended, weight_out, False)
    normed_own = rms_norm(residual, ffn_scale).astype(low)
    normed_ffn = gather_group(normed_own)
    gate_up = dot(normed_ffn, weight_ffn, ((1,), (0,)))
    gate_values, up_values = gate_up[:, :576], gate_up[:, 576:]
    hidden = swiglu(gate_values, up_values).astype(low)

    grad_hidden = dot(group_cotangent, weight_down, ((1,), (1,)))
    _, swiglu_pull = jax.vjp(swiglu, gate_values, up_values)
    grad_gate_up = jnp.concatenate(swiglu_pull(grad_hidden), axis=1).astype(low)
    grad_normed_ffn = multiply_scatter(grad_gate_up, weight_ffn, True)
    grad_w_ffn = dot(normed_ffn, grad_gate_up, ((0,), (0,))).astype(low)
    grad_w_ffn = grad_w_ffn.reshape(16, 8, 8, 1152).transpose(1, 0, 2, 3).reshape(8, 128, 1152)
    grad_w_ffn = lax.all_to_all(grad_w_ffn, "seq", 0, 0, tiled=True)
    _, ffn_pull = jax.vjp(rms_norm, residual, ffn_scale)
    grad_residual, grad_ffn_gain = ffn_pull(grad_normed_ffn)
    grad_residual = grad_residual + cotangent[0].astype(wide)
    grad_branch = gather_group(grad_residual.astype(low))
    grad_branch, hidden = tie(grad_branch, hidden)

    grad_attended = dot(grad_branch, weight_out, ((1,), (1,))).astype(low)
    grad_attended, grad_w_ffn = tie(grad_attended, grad_w_ffn)
    grad_heads = lax.all_to_all(grad_attended, "seq", 0, 0, tiled=True)
    grad_rows = jnp.concatenate(
        [
            dot(hidden, group_cotangent, ((0,), (0,))).astype(low),
            dot(attended, grad_branch, ((0,), (0,))).astype(low),
        ]
    )
    grad_rows = grad_rows.reshape(704, 8, 128).transpose(1, 0, 2)
    grad_rows = lax.all_to_all(grad_rows, "seq", 0, 0, tiled=True)
    block_out = (residual + multiply_scatter(hidden, weight_down, False)).astype(low)[None]

    ffn_sums = grad_w_ffn.astype(wide).sum(0).reshape(2, 64, 1152)
    ffn_send = jnp.where(half == 0, ffn_sums[1], ffn_sums[0]).astype(low)
    ffn_sums = jnp.where(half == 0, ffn_sums[0], ffn_sums[1]) + lax.ppermute(
        ffn_send, "shard", HALF_SWAP
    ).astype(wide)
    ffn_shares = lax.all_to_all(
        ffn_sums.astype(low), "shard", 0, 0, axis_index_groups=GROUPS, tiled=True
    )

    back = attend_back(heads, grad_heads, log_totals)
    back, ffn_shares, grad_rows, block_out = tie(back, ffn_shares, grad_rows, block_out)
    back = lax.all_to_all(back, "seq", 0, 0, tiled=True)

    row_sums = grad_rows.astype(wide).sum(0)
    down_sums, out_sums = row_sums[:576].reshape(2, 288, 128), row_sums[576:].reshape(2, 64, 128)
    out_keep = jnp.where(core == 0, out_sums[0], out_sums[1])
    out_arrived = swap_cores(
        jnp.where(core == 0, out_sums[1], out_sums[0]).astype(low)
    ).astype(wide)
    first = jnp.where(core == 0, out_keep, out_arrived)
    second = jnp.where(core == 0, out_arrived, out_keep)
    first, second = (
        jnp.concatenate([down_sums[0], first]),
        jnp.concatenate([down_sums[1], second]),
    )
    rows_arrived = lax.ppermute(
        jnp.where(half == 0, second, first).astype(low), "shard", HALF_SWAP
    )
    row_shares = (jnp.where(half == 0, first, second) + rows_arrived.astype(wide)).astype(low)
    down_share = row_shares[:288].reshape(9, 32, 128).transpose(1, 0, 2).reshape(32, 1152)
    out_share = row_shares[288:].reshape(8, 8, 128).transpose(1, 0, 2).reshape(8, 1024)
    shares = jnp.concatenate(
        [ffn_shares, down_share, jnp.pad(out_share, ((0, 0), (0, 128)))]
    )
    shares = lax.all_to_all(
        jnp.broadcast_to(shares[None], (8, 104, 1152)), "seq", 0, 0, tiled=True
    )

    _, rope_pull = jax.vjp(rope_local, query_raw, key_raw, q_scale, k_scale)
    grad_query_raw, grad_key_raw, grad_q_gain, grad_k_gain = rope_pull(
        (back[:, :128].astype(wide), back[:, 128:192].astype(wide))
    )
    grad_raw = jnp.concatenate(
        [grad_query_raw.astype(low), grad_key_raw.astype(low), back[:, 192:]], axis=1
    )
    grad_w_qkv = dot(normed, grad_raw, ((0,), (0,))).astype(low)
    grad_attn_gain = (dot(grad_raw, weight_qkv, ((1,), (1,))) * scaled).sum(0)

    grad_gains = jnp.concatenate(
        [
            grad_attn_gain.reshape(16, 64),
            grad_ffn_gain.reshape(16, 64),
            grad_q_gain.reshape(16, 4),
            grad_k_gain.reshape(16, 4),
        ],
        axis=1,
    ).astype(low)
    grad_gains = jnp.pad(grad_gains, ((0, 0), (0, 1024 - 136))).reshape(16, 8, 128)
    grad_columns = jnp.concatenate(
        [
            grad_w_qkv.reshape(16, 8, 8, 256).transpose(1, 0, 2, 3),
            jnp.broadcast_to(grad_gains[None], (8, 16, 8, 128)),
        ],
        axis=3,
    ).reshape(128, 8, 384)
    grad_columns = lax.all_to_all(grad_columns, ("seq", "shard"), 0, 0, tiled=True)
    grad_columns = grad_columns.reshape(16, 8, 8, 384)
    grad_columns = grad_columns.astype(wide).sum(0)
    gain_sums = grad_columns[:, :, 256:].sum(0).reshape(-1)
    head_shares = grad_columns[:, :, :256].reshape(64, 256).astype(low)
    head_shares, shares = tie(head_shares, shares)
    head_shares = lax.all_to_all(
        jnp.broadcast_to(head_shares[None], (8, 64, 256)), "seq", 0, 0, tiled=True
    )

    grad_normed = multiply_scatter(grad_raw, weight_qkv, True)
    _, attn_pull = jax.vjp(lambda values: rms_norm(values, attn_scale), inputs)
    (grad_inputs,) = attn_pull(grad_normed)
    grad_tokens = (grad_inputs + grad_residual).astype(low)[None]

    grad_w_gate, grad_w_up, grad_w_down, grad_w_out = call(
        unpack_ffn_kernel,
        tuple(
            jax.ShapeDtypeStruct(shape, wide)
            for shape in ((64, 4608), (64, 4608), (288, width), (64, width))
        ),
        shares,
    )
    grad_w_query, grad_w_key, grad_w_value = call(
        unpack_heads_kernel,
        tuple(jax.ShapeDtypeStruct((64, size), wide) for size in (width, 512, 512)),
        head_shares,
    )
    return (
        block_out,
        grad_tokens,
        gain_sums[:64],
        grad_w_query,
        grad_w_key,
        grad_w_value,
        gain_sums[128:132],
        gain_sums[132:136],
        grad_w_out,
        gain_sums[64:128],
        grad_w_gate,
        grad_w_up,
        grad_w_down,
    )


def solution(mesh):
    placed = (
        P("shard", "seq", None),
        P("shard"),
        P("shard", None),
        P("shard", None),
        P("shard", None),
        P("shard"),
        P("shard"),
        P("shard", None),
        P("shard"),
        P("shard", None),
        P("shard", None),
        P("shard", None),
        P("shard", "seq", None),
    )
    return jax.shard_map(
        per_device,
        mesh=mesh,
        in_specs=placed,
        out_specs=(
            P("shard", "seq", None),
            P("shard", "seq", None),
            P("shard"),
            P("shard", None),
            P("shard", None),
            P("shard", None),
            P("shard"),
            P("shard"),
            P("shard", None),
            P("shard"),
            P("shard", None),
            P("shard", None),
            P("shard", None),
        ),
        check_vma=False,
    )
```

```python
from functools import partial

import jax
import jax.numpy as jnp
from jax import lax
from jax.experimental import pallas as pl
from jax.experimental.pallas import tpu as pltpu
from jax.sharding import PartitionSpec as P

HEAD_DIM = 64


EPS = 1e-05
THETA = 1000000.0


def rms_norm(values, weight):
    inverse = lax.rsqrt(jnp.mean(values * values, axis=-1, keepdims=True) + EPS)
    return values * inverse * weight


def rope_tables(positions):
    steps_half = jnp.arange(HEAD_DIM // 2).astype(jnp.float32)
    inverse = jnp.exp(-jnp.log(THETA) * 2.0 * steps_half / HEAD_DIM)
    angles = positions[:, None] * inverse[None, :]
    angles = jnp.concatenate([angles, angles], axis=-1)
    return (jnp.cos(angles), jnp.sin(angles))


def rotate(values, cosine_table, sine_table):
    midpoint = values.shape[-1] // 2
    turned = jnp.concatenate([-values[..., midpoint:], values[..., :midpoint]], axis=-1)
    return values * cosine_table[:, None, :] + turned * sine_table[:, None, :]


def qk_local(query_raw, key_raw, q_scale, k_scale, cosine_table, sine_table):
    row_count = query_raw.shape[0]
    queries = rotate(
        rms_norm(query_raw.reshape(row_count, -1, HEAD_DIM), q_scale), cosine_table, sine_table
    )
    key_rows = rotate(
        rms_norm(key_raw.reshape(row_count, -1, HEAD_DIM), k_scale), cosine_table, sine_table
    )
    return (queries.reshape(row_count, -1), key_rows.reshape(row_count, -1))


def swiglu(gate_values, up_values):
    return jax.nn.silu(gate_values) * up_values


def dot(left, right, contract):
    return lax.dot_general(left, right, (contract, ((), ())), preferred_element_type=jnp.float32)


BLOCK = 256


def scores_block(query, keys, first):
    scores = dot(keys, query, ((1,), (1,)))
    key_index = lax.broadcasted_iota(jnp.int32, scores.shape, 0)
    query_index = first + lax.broadcasted_iota(jnp.int32, scores.shape, 1)
    return jnp.where(key_index <= query_index, scores, -1e30)


def head_lanes(head):
    return slice(head * HEAD_DIM, (head + 1) * HEAD_DIM)


def attend_kernel(heads_ref, out_ref, lse_ref):
    length = heads_ref.shape[0]
    values_turned = heads_ref[:, 192:].T
    for first in range(0, length, BLOCK):
        end = first + BLOCK
        keys = heads_ref[:end, 128:192]
        parts = []
        for head in range(2):
            query = heads_ref[first:end, head * HEAD_DIM : (head + 1) * HEAD_DIM] * 0.125
            scores = scores_block(query, keys, first)
            row_max = jnp.max(scores, axis=0, keepdims=True)
            exponent = jnp.exp(scores - row_max)
            row_sum = jnp.sum(exponent, axis=0, keepdims=True)
            parts.append(
                dot(values_turned[:, :end], exponent.astype(jnp.bfloat16), ((1,), (0,))) / row_sum
            )
            lse_ref[head : head + 1, first:end] = row_max + jnp.log(row_sum)
        out_ref[first:end, :] = jnp.concatenate(parts).T.astype(jnp.bfloat16)


def attend_back_kernel(heads_ref, grad_ref, lse_ref, out_ref, keys_total, values_total):
    length = heads_ref.shape[0]
    keys_turned = heads_ref[:, 128:192].T
    keys_total[...] = jnp.zeros_like(keys_total)
    values_total[...] = jnp.zeros_like(values_total)
    for first in range(0, length, BLOCK):
        end = first + BLOCK
        keys = heads_ref[:end, 128:192]
        values = heads_ref[:end, 192:]
        parts = []
        for head in range(2):
            lanes = slice(head * HEAD_DIM, (head + 1) * HEAD_DIM)
            query = heads_ref[first:end, lanes] * 0.125
            grad = grad_ref[first:end, lanes]
            exact = jnp.exp(
                scores_block(query, keys, first) - lse_ref[head : head + 1, first:end]
            )
            grad_probs = dot(values, grad, ((1,), (1,)))
            inner = jnp.sum(exact * grad_probs, axis=0, keepdims=True)
            grad_scores = (exact * (grad_probs - inner)).astype(jnp.bfloat16)
            parts.append(dot(keys_turned[:, :end], grad_scores, ((1,), (0,))) * 0.125)
            keys_total[:end, :] += dot(grad_scores, query, ((1,), (0,)))
            values_total[:end, :] += dot(exact.astype(jnp.bfloat16), grad, ((1,), (0,)))
        out_ref[first:end, :128] = jnp.concatenate(parts).T.astype(jnp.bfloat16)
    out_ref[:, 128:] = jnp.concatenate([keys_total[...], values_total[...]], axis=1).astype(
        jnp.bfloat16
    )


VMEM = pl.BlockSpec(memory_space=pltpu.VMEM)


def attend(heads):
    length = heads.shape[0]
    return pl.pallas_call(
        attend_kernel,
        out_shape=(
            jax.ShapeDtypeStruct((length, 128), jnp.bfloat16),
            jax.ShapeDtypeStruct((2, length), jnp.float32),
        ),
        in_specs=[VMEM],
        out_specs=(VMEM, VMEM),
        compiler_params=pltpu.CompilerParams(vmem_limit_bytes=32 * 2**20),
        cost_estimate=pl.CostEstimate(
            flops=5 * 10**8, bytes_accessed=2**20, transcendentals=2 * length * length
        ),
    )(heads)


def attend_back(heads, grad_heads, log_totals):
    length = heads.shape[0]
    return pl.pallas_call(
        attend_back_kernel,
        out_shape=jax.ShapeDtypeStruct((length, 256), jnp.bfloat16),
        in_specs=[VMEM] * 3,
        out_specs=VMEM,
        scratch_shapes=[pltpu.VMEM((length, HEAD_DIM), jnp.float32)] * 2,
        compiler_params=pltpu.CompilerParams(vmem_limit_bytes=32 * 2**20),
        cost_estimate=pl.CostEstimate(
            flops=10**9, bytes_accessed=2**20, transcendentals=2 * length * length
        ),
    )(heads, grad_heads, log_totals)


def call(kernel, out_shape, *operands, flops=10**6):
    several = isinstance(out_shape, tuple)
    return pl.pallas_call(
        kernel,
        out_shape=out_shape,
        in_specs=[VMEM] * len(operands),
        out_specs=(VMEM,) * len(out_shape) if several else VMEM,
        compiler_params=pltpu.CompilerParams(vmem_limit_bytes=48 * 2**20),
        cost_estimate=pl.CostEstimate(flops=flops, bytes_accessed=2**20, transcendentals=0),
    )(*operands)


def stack_kernel(*refs):
    *pieces, out_ref = refs
    row = 0
    for piece in pieces:
        out_ref[row : row + piece.shape[0], :] = piece[...]
        row += piece.shape[0]


def stack_rows(*pieces):
    rows = sum(piece.shape[0] for piece in pieces)
    return call(
        stack_kernel, jax.ShapeDtypeStruct((rows, pieces[0].shape[1]), pieces[0].dtype), *pieces
    )


def head_index(place):
    return place % 2 * 4 + place // 2


def pack_heads_kernel(query_ref, key_ref, value_ref, gain_ref, out_ref):
    for place in range(8):
        head = head_index(place)
        narrow = slice(head * HEAD_DIM, (head + 1) * HEAD_DIM)
        block = jnp.concatenate(
            [
                query_ref[:, head * 128 : (head + 1) * 128],
                key_ref[:, narrow],
                value_ref[:, narrow],
            ],
            axis=1,
        )
        for half in range(2):
            out_ref[half * 8 + place, :64, :] = block
            out_ref[half * 8 + place, 64:, :] = gain_ref[...]


def pack_ffn_kernel(gate_ref, up_ref, out_ref):
    for place in range(8):
        low, high = place * 288, (8 + place) * 288
        out_ref[place] = jnp.concatenate(
            [
                gate_ref[:, low : low + 288],
                gate_ref[:, high : high + 288],
                up_ref[:, low : low + 288],
                up_ref[:, high : high + 288],
            ],
            axis=1,
        )


def unpack_kernel(
    share_ref, gate_ref, up_ref, down_ref, out_ref, query_ref, key_ref, value_ref
):
    for place in range(8):
        block = share_ref[:, place * 8 : place * 8 + 8, :].astype(jnp.float32).reshape(64, 1152)
        low, high = place * 288, (8 + place) * 288
        gate_ref[:, low : low + 288] = block[:, :288]
        gate_ref[:, high : high + 288] = block[:, 288:576]
        up_ref[:, low : low + 288] = block[:, 576:864]
        up_ref[:, high : high + 288] = block[:, 864:]
        head = head_index(place)
        lanes = slice(place // 2 * 256, place // 2 * 256 + 256)
        start = 104 + place % 2 * 8
        block = share_ref[:, start : start + 8, lanes].astype(jnp.float32).reshape(64, 256)
        query_ref[:, head * 128 : (head + 1) * 128] = block[:, :128]
        key_ref[:, head_lanes(head)] = block[:, 128:192]
        value_ref[:, head_lanes(head)] = block[:, 192:]
    for part in range(8):
        lanes = slice(part * 128, (part + 1) * 128)
        for piece in range(9):
            down_ref[piece * 32 : (piece + 1) * 32, lanes] = share_ref[
                part, 64:96, piece * 128 : (piece + 1) * 128
            ].astype(jnp.float32)
        for piece in range(8):
            out_ref[piece * 8 : (piece + 1) * 8, lanes] = share_ref[
                part, 96:104, piece * 128 : (piece + 1) * 128
            ].astype(jnp.float32)


def near_kernel(turned, left_ref, right_ref, far_ref, own_ref, *send_refs):
    rows = own_ref.shape[0]
    total = dot(left_ref[:512, :], right_ref[...], ((1,), (1 if turned else 0,)))
    total = total + far_ref[...].astype(jnp.float32)
    own_ref[...] = total[:rows]
    for step, send_ref in enumerate(send_refs, 1):
        send_ref[...] = total[step * rows : (step + 1) * rows].astype(jnp.bfloat16)


def y_perm(step):
    return [
        (half * 8 + ((y + step) % 4) * 2 + core, half * 8 + y * 2 + core)
        for half in range(2)
        for y in range(4)
        for core in range(2)
    ]


CORE_SWAP = [(index, index ^ 1) for index in range(16)]
HALF_SWAP = [(index, index ^ 8) for index in range(16)]
GROUPS = [list(range(8)), list(range(8, 16))]


def swap_cores(block):
    return lax.ppermute(block, "shard", CORE_SWAP)


def gather_group(block):
    near = [block] + [lax.ppermute(block, "shard", y_perm(step)) for step in (1, 2, 3)]
    return stack_rows(*near, *[swap_cores(piece) for piece in near])


def multiply_scatter(left, right, turned):
    far = dot(left[512:], right, ((1,), (1 if turned else 0,)))
    far = swap_cores(far.astype(jnp.bfloat16))
    width = far.shape[1]
    wide, low = (
        jax.ShapeDtypeStruct((128, width), dtype) for dtype in (jnp.float32, jnp.bfloat16)
    )
    total, *sends = call(
        partial(near_kernel, turned),
        (wide, low, low, low),
        left,
        right,
        far,
        flops=2 * 512 * left.shape[1] * width,
    )
    for step, send in enumerate(sends, 1):
        arrived = lax.ppermute(send, "shard", y_perm(4 - step))
        total = total + arrived.astype(jnp.float32)
    return total


def both_halves(block, half):
    other = lax.ppermute(block, "shard", HALF_SWAP)
    first = half == 0
    return jnp.stack([jnp.where(first, block, other), jnp.where(first, other, block)])


def tie(*arrays):
    return lax.optimization_barrier(arrays)


def per_device(
    tokens,
    attn_gain,
    w_query,
    w_key,
    w_value,
    q_gain,
    k_gain,
    w_out,
    ffn_gain,
    w_gate,
    w_up,
    w_down,
    cotangent,
):
    low, wide = jnp.bfloat16, jnp.float32
    shard = lax.axis_index("shard")
    half, core = shard // 8, shard % 2
    own_tokens = tokens[0]
    rows, width = own_tokens.shape
    group_tokens = gather_group(own_tokens)

    gains = jnp.concatenate([attn_gain, ffn_gain, q_gain, k_gain])
    gain_rows = jnp.broadcast_to(jnp.pad(gains, (0, 120))[None], (16, 256))
    head_columns = call(
        pack_heads_kernel,
        jax.ShapeDtypeStruct((16, 80, 256), low),
        w_query,
        w_key,
        w_value,
        gain_rows,
    )
    head_columns = lax.all_to_all(head_columns, "shard", 0, 0, tiled=True)
    gain_all = head_columns[:, 64, :136].astype(wide)
    attn_scale = gain_all[:, :64].reshape(-1)
    ffn_scale = gain_all[:, 64:128].reshape(-1)
    q_scale = gain_all[:, 128:132].reshape(-1)
    k_scale = gain_all[:, 132:136].reshape(-1)
    weight_qkv = head_columns[:, :64].reshape(width, 256)

    positions = (lax.axis_index("seq") * rows + jnp.arange(rows, dtype=jnp.int32)).astype(wide)
    cosine_table, sine_table = (jnp.tile(table, (8, 1)) for table in rope_tables(positions))
    rope_local = partial(qk_local, cosine_table=cosine_table, sine_table=sine_table)
    wide_tokens = group_tokens.astype(wide)
    scaled = wide_tokens * lax.rsqrt(
        jnp.mean(wide_tokens * wide_tokens, axis=-1, keepdims=True) + EPS
    )
    normed = (scaled * attn_scale).astype(low)
    raw = dot(normed, weight_qkv, ((1,), (0,)))
    query_raw, key_raw, value_raw = raw[:, :128], raw[:, 128:192], raw[:, 192:]
    query_rot, key_rot = rope_local(query_raw, key_raw, q_scale, k_scale)
    heads = jnp.concatenate([query_rot, key_rot, value_raw], axis=1).astype(low)

    ffn_columns = call(
        pack_ffn_kernel, jax.ShapeDtypeStruct((8, 64, 1152), low), w_gate, w_up
    )
    ffn_columns = lax.all_to_all(
        ffn_columns, "shard", 0, 0, axis_index_groups=GROUPS, tiled=True
    )
    weight_down = both_halves(w_down, half).reshape(576, width)
    out_halves = both_halves(w_out, half)
    out_own = jnp.where(core == 0, out_halves[0], out_halves[1])
    out_other = swap_cores(jnp.where(core == 0, out_halves[1], out_halves[0]))
    weight_out = jnp.concatenate(
        [jnp.where(core == 0, out_own, out_other), jnp.where(core == 0, out_other, out_own)]
    )

    heads = lax.all_to_all(heads, "seq", 0, 0, tiled=True)
    attended, log_totals = attend(heads)
    attended, ffn_columns, weight_down, weight_out = tie(
        attended, ffn_columns, weight_down, weight_out
    )
    weight_ffn = both_halves(ffn_columns, half).reshape(width, 1152)
    group_cotangent = gather_group(cotangent[0])
    attended = lax.all_to_all(attended, "seq", 0, 0, tiled=True)
    attended, group_cotangent = tie(attended, group_cotangent)

    inputs = own_tokens.astype(wide)
    residual = inputs + multiply_scatter(attended, weight_out, False)
    normed_own = rms_norm(residual, ffn_scale).astype(low)
    normed_ffn = gather_group(normed_own)
    gate_up = dot(normed_ffn, weight_ffn, ((1,), (0,)))
    gate_values, up_values = gate_up[:, :576], gate_up[:, 576:]
    hidden = swiglu(gate_values, up_values).astype(low)

    grad_hidden = dot(group_cotangent, weight_down, ((1,), (1,)))
    _, swiglu_pull = jax.vjp(swiglu, gate_values, up_values)
    grad_gate_up = jnp.concatenate(swiglu_pull(grad_hidden), axis=1).astype(low)
    grad_normed_ffn = multiply_scatter(grad_gate_up, weight_ffn, True)
    grad_w_ffn = dot(normed_ffn, grad_gate_up, ((0,), (0,))).astype(low)
    grad_w_ffn = grad_w_ffn.reshape(16, 8, 8, 1152).transpose(1, 0, 2, 3).reshape(8, 128, 1152)
    grad_w_ffn = lax.all_to_all(grad_w_ffn, "seq", 0, 0, tiled=True)
    _, ffn_pull = jax.vjp(rms_norm, residual, ffn_scale)
    grad_residual, grad_ffn_gain = ffn_pull(grad_normed_ffn)
    grad_residual = grad_residual + cotangent[0].astype(wide)
    grad_branch = gather_group(grad_residual.astype(low))
    grad_branch, hidden = tie(grad_branch, hidden)

    grad_attended = dot(grad_branch, weight_out, ((1,), (1,))).astype(low)
    grad_attended, grad_w_ffn = tie(grad_attended, grad_w_ffn)
    grad_heads = lax.all_to_all(grad_attended, "seq", 0, 0, tiled=True)
    grad_rows = jnp.concatenate(
        [
            dot(hidden, group_cotangent, ((0,), (0,))).astype(low),
            dot(attended, grad_branch, ((0,), (0,))).astype(low),
        ]
    )
    grad_rows = grad_rows.reshape(704, 8, 128).transpose(1, 0, 2)
    grad_rows = lax.all_to_all(grad_rows, "seq", 0, 0, tiled=True)
    block_out = (residual + multiply_scatter(hidden, weight_down, False)).astype(low)[None]

    ffn_sums = grad_w_ffn.astype(wide).sum(0).reshape(2, 64, 1152)
    ffn_send = jnp.where(half == 0, ffn_sums[1], ffn_sums[0]).astype(low)
    ffn_sums = jnp.where(half == 0, ffn_sums[0], ffn_sums[1]) + lax.ppermute(
        ffn_send, "shard", HALF_SWAP
    ).astype(wide)
    ffn_shares = lax.all_to_all(
        ffn_sums.astype(low), "shard", 0, 0, axis_index_groups=GROUPS, tiled=True
    )

    back = attend_back(heads, grad_heads, log_totals)
    back, ffn_shares, grad_rows, block_out = tie(back, ffn_shares, grad_rows, block_out)
    back = lax.all_to_all(back, "seq", 0, 0, tiled=True)

    row_sums = grad_rows.astype(wide).sum(0)
    down_sums, out_sums = row_sums[:576].reshape(2, 288, 128), row_sums[576:].reshape(2, 64, 128)
    out_keep = jnp.where(core == 0, out_sums[0], out_sums[1])
    out_arrived = swap_cores(
        jnp.where(core == 0, out_sums[1], out_sums[0]).astype(low)
    ).astype(wide)
    first = jnp.where(core == 0, out_keep, out_arrived)
    second = jnp.where(core == 0, out_arrived, out_keep)
    first, second = (
        jnp.concatenate([down_sums[0], first]),
        jnp.concatenate([down_sums[1], second]),
    )
    rows_arrived = lax.ppermute(
        jnp.where(half == 0, second, first).astype(low), "shard", HALF_SWAP
    )
    row_shares = (jnp.where(half == 0, first, second) + rows_arrived.astype(wide)).astype(low)
    down_share = row_shares[:288].reshape(9, 32, 128).transpose(1, 0, 2).reshape(32, 1152)
    out_share = row_shares[288:].reshape(8, 8, 128).transpose(1, 0, 2).reshape(8, 1024)
    _, rope_pull = jax.vjp(rope_local, query_raw, key_raw, q_scale, k_scale)
    grad_query_raw, grad_key_raw, grad_q_gain, grad_k_gain = rope_pull(
        (back[:, :128].astype(wide), back[:, 128:192].astype(wide))
    )
    grad_raw = jnp.concatenate(
        [grad_query_raw.astype(low), grad_key_raw.astype(low), back[:, 192:]], axis=1
    )
    grad_w_qkv = dot(normed, grad_raw, ((0,), (0,))).astype(low)
    grad_attn_gain = (dot(grad_raw, weight_qkv, ((1,), (1,))) * scaled).sum(0)

    grad_gains = jnp.concatenate(
        [
            grad_attn_gain.reshape(16, 64),
            grad_ffn_gain.reshape(16, 64),
            grad_q_gain.reshape(16, 4),
            grad_k_gain.reshape(16, 4),
        ],
        axis=1,
    ).astype(low)
    grad_gains = jnp.pad(grad_gains, ((0, 0), (0, 1024 - 136))).reshape(16, 8, 128)
    grad_columns = jnp.concatenate(
        [
            grad_w_qkv.reshape(16, 8, 8, 256).transpose(1, 0, 2, 3),
            jnp.broadcast_to(grad_gains[None], (8, 16, 8, 128)),
        ],
        axis=3,
    ).reshape(128, 8, 384)
    grad_columns = lax.all_to_all(grad_columns, ("seq", "shard"), 0, 0, tiled=True)
    grad_columns = grad_columns.reshape(16, 8, 8, 384)
    grad_columns = grad_columns.astype(wide).sum(0)
    gain_sums = grad_columns[:, :, 256:].sum(0).reshape(-1)
    head_shares = grad_columns[:, :, :256].astype(low)
    head_shares = head_shares.reshape(4, 16, 256).transpose(1, 0, 2).reshape(16, 1024)
    shares = jnp.concatenate(
        [
            ffn_shares.reshape(64, 1152),
            down_share,
            jnp.pad(jnp.concatenate([out_share, head_shares]), ((0, 0), (0, 128))),
        ]
    )
    shares = lax.all_to_all(
        jnp.broadcast_to(shares[None], (8,) + shares.shape), "seq", 0, 0, tiled=True
    )

    grad_normed = multiply_scatter(grad_raw, weight_qkv, True)
    _, attn_pull = jax.vjp(lambda values: rms_norm(values, attn_scale), inputs)
    (grad_inputs,) = attn_pull(grad_normed)
    grad_tokens = (grad_inputs + grad_residual).astype(low)[None]

    grad_w_gate, grad_w_up, grad_w_down, grad_w_out, grad_w_query, grad_w_key, grad_w_value = call(
        unpack_kernel,
        tuple(
            jax.ShapeDtypeStruct(shape, wide)
            for shape in (
                (64, 4608),
                (64, 4608),
                (288, width),
                (64, width),
                (64, width),
                (64, 512),
                (64, 512),
            )
        ),
        shares,
    )
    return (
        block_out,
        grad_tokens,
        gain_sums[:64],
        grad_w_query,
        grad_w_key,
        grad_w_value,
        gain_sums[128:132],
        gain_sums[132:136],
        grad_w_out,
        gain_sums[64:128],
        grad_w_gate,
        grad_w_up,
        grad_w_down,
    )


def solution(mesh):
    placed = (
        P("shard", "seq", None),
        P("shard"),
        P("shard", None),
        P("shard", None),
        P("shard", None),
        P("shard"),
        P("shard"),
        P("shard", None),
        P("shard"),
        P("shard", None),
        P("shard", None),
        P("shard", None),
        P("shard", "seq", None),
    )
    return jax.shard_map(
        per_device,
        mesh=mesh,
        in_specs=placed,
        out_specs=(
            P("shard", "seq", None),
            P("shard", "seq", None),
            P("shard"),
            P("shard", None),
            P("shard", None),
            P("shard", None),
            P("shard"),
            P("shard"),
            P("shard", None),
            P("shard"),
            P("shard", None),
            P("shard", None),
            P("shard", None),
        ),
        check_vma=False,
    )
```

```python
from functools import partial

import jax
import jax.numpy as jnp
from jax import lax
from jax.experimental import pallas as pl
from jax.experimental.pallas import tpu as pltpu
from jax.sharding import PartitionSpec as P

HEAD_DIM = 64


EPS = 1e-05
THETA = 1000000.0


def rms_norm(values, weight):
    inverse = lax.rsqrt(jnp.mean(values * values, axis=-1, keepdims=True) + EPS)
    return values * inverse * weight


def rope_tables(positions):
    steps_half = jnp.arange(HEAD_DIM // 2).astype(jnp.float32)
    inverse = jnp.exp(-jnp.log(THETA) * 2.0 * steps_half / HEAD_DIM)
    angles = positions[:, None] * inverse[None, :]
    angles = jnp.concatenate([angles, angles], axis=-1)
    return (jnp.cos(angles), jnp.sin(angles))


def rotate(values, cosine_table, sine_table):
    midpoint = values.shape[-1] // 2
    turned = jnp.concatenate([-values[..., midpoint:], values[..., :midpoint]], axis=-1)
    return values * cosine_table[:, None, :] + turned * sine_table[:, None, :]


def qk_local(query_raw, key_raw, q_scale, k_scale, cosine_table, sine_table):
    row_count = query_raw.shape[0]
    queries = rotate(
        rms_norm(query_raw.reshape(row_count, -1, HEAD_DIM), q_scale), cosine_table, sine_table
    )
    key_rows = rotate(
        rms_norm(key_raw.reshape(row_count, -1, HEAD_DIM), k_scale), cosine_table, sine_table
    )
    return (queries.reshape(row_count, -1), key_rows.reshape(row_count, -1))


def swiglu(gate_values, up_values):
    return jax.nn.silu(gate_values) * up_values


def dot(left, right, contract):
    return lax.dot_general(left, right, (contract, ((), ())), preferred_element_type=jnp.float32)


BLOCK = 256


def scores_block(query, keys, first):
    scores = dot(keys, query, ((1,), (1,)))
    key_index = lax.broadcasted_iota(jnp.int32, scores.shape, 0)
    query_index = first + lax.broadcasted_iota(jnp.int32, scores.shape, 1)
    return jnp.where(key_index <= query_index, scores, -1e30)


def head_lanes(head):
    return slice(head * HEAD_DIM, (head + 1) * HEAD_DIM)


def attend_kernel(heads_ref, out_ref, lse_ref):
    length = heads_ref.shape[0]
    values_turned = heads_ref[:, 192:].T
    for first in range(0, length, BLOCK):
        end = first + BLOCK
        keys = heads_ref[:end, 128:192]
        parts = []
        for head in range(2):
            query = heads_ref[first:end, head * HEAD_DIM : (head + 1) * HEAD_DIM] * 0.125
            scores = scores_block(query, keys, first)
            row_max = jnp.max(scores, axis=0, keepdims=True)
            exponent = jnp.exp(scores - row_max)
            row_sum = jnp.sum(exponent, axis=0, keepdims=True)
            parts.append(
                dot(values_turned[:, :end], exponent.astype(jnp.bfloat16), ((1,), (0,))) / row_sum
            )
            lse_ref[head : head + 1, first:end] = row_max + jnp.log(row_sum)
        out_ref[first:end, :] = jnp.concatenate(parts).T.astype(jnp.bfloat16)


def attend_back_kernel(heads_ref, grad_ref, lse_ref, out_ref, keys_total, values_total):
    length = heads_ref.shape[0]
    keys_turned = heads_ref[:, 128:192].T
    keys_total[...] = jnp.zeros_like(keys_total)
    values_total[...] = jnp.zeros_like(values_total)
    for first in range(0, length, BLOCK):
        end = first + BLOCK
        keys = heads_ref[:end, 128:192]
        values = heads_ref[:end, 192:]
        parts = []
        for head in range(2):
            lanes = slice(head * HEAD_DIM, (head + 1) * HEAD_DIM)
            query = heads_ref[first:end, lanes] * 0.125
            grad = grad_ref[first:end, lanes]
            exact = jnp.exp(
                scores_block(query, keys, first) - lse_ref[head : head + 1, first:end]
            )
            grad_probs = dot(values, grad, ((1,), (1,)))
            inner = jnp.sum(exact * grad_probs, axis=0, keepdims=True)
            grad_scores = (exact * (grad_probs - inner)).astype(jnp.bfloat16)
            parts.append(dot(keys_turned[:, :end], grad_scores, ((1,), (0,))) * 0.125)
            keys_total[:end, :] += dot(grad_scores, query, ((1,), (0,)))
            values_total[:end, :] += dot(exact.astype(jnp.bfloat16), grad, ((1,), (0,)))
        out_ref[first:end, :128] = jnp.concatenate(parts).T.astype(jnp.bfloat16)
    out_ref[:, 128:] = jnp.concatenate([keys_total[...], values_total[...]], axis=1).astype(
        jnp.bfloat16
    )


VMEM = pl.BlockSpec(memory_space=pltpu.VMEM)


def attend(heads):
    length = heads.shape[0]
    return pl.pallas_call(
        attend_kernel,
        out_shape=(
            jax.ShapeDtypeStruct((length, 128), jnp.bfloat16),
            jax.ShapeDtypeStruct((2, length), jnp.float32),
        ),
        in_specs=[VMEM],
        out_specs=(VMEM, VMEM),
        compiler_params=pltpu.CompilerParams(vmem_limit_bytes=16 * 2**20),
        cost_estimate=pl.CostEstimate(
            flops=5 * 10**8, bytes_accessed=2**20, transcendentals=2 * length * length
        ),
    )(heads)


def attend_back(heads, grad_heads, log_totals):
    length = heads.shape[0]
    return pl.pallas_call(
        attend_back_kernel,
        out_shape=jax.ShapeDtypeStruct((length, 256), jnp.bfloat16),
        in_specs=[VMEM] * 3,
        out_specs=VMEM,
        scratch_shapes=[pltpu.VMEM((length, HEAD_DIM), jnp.float32)] * 2,
        compiler_params=pltpu.CompilerParams(vmem_limit_bytes=16 * 2**20),
        cost_estimate=pl.CostEstimate(
            flops=10**9, bytes_accessed=2**20, transcendentals=2 * length * length
        ),
    )(heads, grad_heads, log_totals)


def call(kernel, out_shape, *operands, flops=10**6):
    several = isinstance(out_shape, tuple)
    return pl.pallas_call(
        kernel,
        out_shape=out_shape,
        in_specs=[VMEM] * len(operands),
        out_specs=(VMEM,) * len(out_shape) if several else VMEM,
        compiler_params=pltpu.CompilerParams(vmem_limit_bytes=16 * 2**20),
        cost_estimate=pl.CostEstimate(flops=flops, bytes_accessed=2**20, transcendentals=0),
    )(*operands)


def stack_kernel(*refs):
    *pieces, out_ref = refs
    row = 0
    for piece in pieces:
        out_ref[row : row + piece.shape[0], :] = piece[...]
        row += piece.shape[0]


def stack_rows(*pieces):
    rows = sum(piece.shape[0] for piece in pieces)
    return call(
        stack_kernel, jax.ShapeDtypeStruct((rows, pieces[0].shape[1]), pieces[0].dtype), *pieces
    )


def head_index(place):
    return place % 2 * 4 + place // 2


def pack_heads_kernel(query_ref, key_ref, value_ref, gain_ref, out_ref):
    for place in range(8):
        head = head_index(place)
        narrow = slice(head * HEAD_DIM, (head + 1) * HEAD_DIM)
        block = jnp.concatenate(
            [
                query_ref[:, head * 128 : (head + 1) * 128],
                key_ref[:, narrow],
                value_ref[:, narrow],
            ],
            axis=1,
        )
        for half in range(2):
            out_ref[half * 8 + place, :64, :] = block
            out_ref[half * 8 + place, 64:, :] = gain_ref[...]


def pack_ffn_kernel(gate_ref, up_ref, out_ref):
    for place in range(8):
        low, high = place * 288, (8 + place) * 288
        out_ref[place] = jnp.concatenate(
            [
                gate_ref[:, low : low + 288],
                gate_ref[:, high : high + 288],
                up_ref[:, low : low + 288],
                up_ref[:, high : high + 288],
            ],
            axis=1,
        )


def unpack_kernel(
    share_ref, gate_ref, up_ref, down_ref, out_ref, query_ref, key_ref, value_ref
):
    for place in range(8):
        block = share_ref[:, place * 8 : place * 8 + 8, :].astype(jnp.float32).reshape(64, 1152)
        low, high = place * 288, (8 + place) * 288
        gate_ref[:, low : low + 288] = block[:, :288]
        gate_ref[:, high : high + 288] = block[:, 288:576]
        up_ref[:, low : low + 288] = block[:, 576:864]
        up_ref[:, high : high + 288] = block[:, 864:]
        head = head_index(place)
        lanes = slice(place // 2 * 256, place // 2 * 256 + 256)
        start = 104 + place % 2 * 8
        block = share_ref[:, start : start + 8, lanes].astype(jnp.float32).reshape(64, 256)
        query_ref[:, head * 128 : (head + 1) * 128] = block[:, :128]
        key_ref[:, head_lanes(head)] = block[:, 128:192]
        value_ref[:, head_lanes(head)] = block[:, 192:]
    for part in range(8):
        lanes = slice(part * 128, (part + 1) * 128)
        for piece in range(9):
            down_ref[piece * 32 : (piece + 1) * 32, lanes] = share_ref[
                part, 64:96, piece * 128 : (piece + 1) * 128
            ].astype(jnp.float32)
        for piece in range(8):
            out_ref[piece * 8 : (piece + 1) * 8, lanes] = share_ref[
                part, 96:104, piece * 128 : (piece + 1) * 128
            ].astype(jnp.float32)


def near_kernel(turned, left_ref, right_ref, far_ref, own_ref, *send_refs):
    rows = own_ref.shape[0]
    total = dot(left_ref[:512, :], right_ref[...], ((1,), (1 if turned else 0,)))
    total = total + far_ref[...].astype(jnp.float32)
    own_ref[...] = total[:rows]
    for step, send_ref in enumerate(send_refs, 1):
        send_ref[...] = total[step * rows : (step + 1) * rows].astype(jnp.bfloat16)


def y_perm(step):
    return [
        (half * 8 + ((y + step) % 4) * 2 + core, half * 8 + y * 2 + core)
        for half in range(2)
        for y in range(4)
        for core in range(2)
    ]


CORE_SWAP = [(index, index ^ 1) for index in range(16)]
HALF_SWAP = [(index, index ^ 8) for index in range(16)]
GROUPS = [list(range(8)), list(range(8, 16))]


def swap_cores(block):
    return lax.ppermute(block, "shard", CORE_SWAP)


def gather_group(block):
    near = [block] + [lax.ppermute(block, "shard", y_perm(step)) for step in (1, 2, 3)]
    return stack_rows(*near, *[swap_cores(piece) for piece in near])


def multiply_scatter(left, right, turned):
    far = dot(left[512:], right, ((1,), (1 if turned else 0,)))
    far = swap_cores(far.astype(jnp.bfloat16))
    width = far.shape[1]
    wide, low = (
        jax.ShapeDtypeStruct((128, width), dtype) for dtype in (jnp.float32, jnp.bfloat16)
    )
    total, *sends = call(
        partial(near_kernel, turned),
        (wide, low, low, low),
        left,
        right,
        far,
        flops=2 * 512 * left.shape[1] * width,
    )
    for step, send in enumerate(sends, 1):
        arrived = lax.ppermute(send, "shard", y_perm(4 - step))
        total = total + arrived.astype(jnp.float32)
    return total


def both_halves(block, half):
    other = lax.ppermute(block, "shard", HALF_SWAP)
    first = half == 0
    return jnp.stack([jnp.where(first, block, other), jnp.where(first, other, block)])


def tie(*arrays):
    return lax.optimization_barrier(arrays)


def per_device(
    tokens,
    attn_gain,
    w_query,
    w_key,
    w_value,
    q_gain,
    k_gain,
    w_out,
    ffn_gain,
    w_gate,
    w_up,
    w_down,
    cotangent,
):
    low, wide = jnp.bfloat16, jnp.float32
    shard = lax.axis_index("shard")
    half, core = shard // 8, shard % 2
    own_tokens = tokens[0]
    rows, width = own_tokens.shape
    group_tokens = gather_group(own_tokens)

    gains = jnp.concatenate([attn_gain, ffn_gain, q_gain, k_gain])
    gain_rows = jnp.broadcast_to(jnp.pad(gains, (0, 120))[None], (16, 256))
    head_columns = call(
        pack_heads_kernel,
        jax.ShapeDtypeStruct((16, 80, 256), low),
        w_query,
        w_key,
        w_value,
        gain_rows,
    )
    head_columns = lax.all_to_all(head_columns, "shard", 0, 0, tiled=True)
    gain_all = head_columns[:, 64, :136].astype(wide)
    attn_scale = gain_all[:, :64].reshape(-1)
    ffn_scale = gain_all[:, 64:128].reshape(-1)
    q_scale = gain_all[:, 128:132].reshape(-1)
    k_scale = gain_all[:, 132:136].reshape(-1)
    weight_qkv = head_columns[:, :64].reshape(width, 256)

    positions = (lax.axis_index("seq") * rows + jnp.arange(rows, dtype=jnp.int32)).astype(wide)
    cosine_table, sine_table = (jnp.tile(table, (8, 1)) for table in rope_tables(positions))
    rope_local = partial(qk_local, cosine_table=cosine_table, sine_table=sine_table)
    wide_tokens = group_tokens.astype(wide)
    scaled = wide_tokens * lax.rsqrt(
        jnp.mean(wide_tokens * wide_tokens, axis=-1, keepdims=True) + EPS
    )
    normed = (scaled * attn_scale).astype(low)
    raw = dot(normed, weight_qkv, ((1,), (0,)))
    query_raw, key_raw, value_raw = raw[:, :128], raw[:, 128:192], raw[:, 192:]
    query_rot, key_rot = rope_local(query_raw, key_raw, q_scale, k_scale)
    heads = jnp.concatenate([query_rot, key_rot, value_raw], axis=1).astype(low)

    ffn_columns = call(
        pack_ffn_kernel, jax.ShapeDtypeStruct((8, 64, 1152), low), w_gate, w_up
    )
    ffn_columns = lax.all_to_all(
        ffn_columns, "shard", 0, 0, axis_index_groups=GROUPS, tiled=True
    )
    weight_down = both_halves(w_down, half).reshape(576, width)
    out_halves = both_halves(w_out, half)
    out_own = jnp.where(core == 0, out_halves[0], out_halves[1])
    out_other = swap_cores(jnp.where(core == 0, out_halves[1], out_halves[0]))
    weight_out = jnp.concatenate(
        [jnp.where(core == 0, out_own, out_other), jnp.where(core == 0, out_other, out_own)]
    )

    heads = lax.all_to_all(heads, "seq", 0, 0, tiled=True)
    attended, log_totals = attend(heads)
    attended, ffn_columns, weight_down, weight_out = tie(
        attended, ffn_columns, weight_down, weight_out
    )
    weight_ffn = both_halves(ffn_columns, half).reshape(width, 1152)
    group_cotangent = gather_group(cotangent[0])
    attended = lax.all_to_all(attended, "seq", 0, 0, tiled=True)
    attended, group_cotangent = tie(attended, group_cotangent)

    inputs = own_tokens.astype(wide)
    residual = inputs + multiply_scatter(attended, weight_out, False)
    normed_own = rms_norm(residual, ffn_scale).astype(low)
    normed_ffn = gather_group(normed_own)
    gate_up = dot(normed_ffn, weight_ffn, ((1,), (0,)))
    gate_values, up_values = gate_up[:, :576], gate_up[:, 576:]
    hidden = swiglu(gate_values, up_values).astype(low)

    grad_hidden = dot(group_cotangent, weight_down, ((1,), (1,)))
    _, swiglu_pull = jax.vjp(swiglu, gate_values, up_values)
    grad_gate_up = jnp.concatenate(swiglu_pull(grad_hidden), axis=1).astype(low)
    grad_normed_ffn = multiply_scatter(grad_gate_up, weight_ffn, True)
    grad_w_ffn = dot(normed_ffn, grad_gate_up, ((0,), (0,))).astype(low)
    grad_w_ffn = grad_w_ffn.reshape(16, 8, 8, 1152).transpose(1, 0, 2, 3).reshape(8, 128, 1152)
    grad_w_ffn = lax.all_to_all(grad_w_ffn, "seq", 0, 0, tiled=True)
    _, ffn_pull = jax.vjp(rms_norm, residual, ffn_scale)
    grad_residual, grad_ffn_gain = ffn_pull(grad_normed_ffn)
    grad_residual = grad_residual + cotangent[0].astype(wide)
    grad_branch = gather_group(grad_residual.astype(low))
    grad_branch, hidden = tie(grad_branch, hidden)

    grad_attended = dot(grad_branch, weight_out, ((1,), (1,))).astype(low)
    grad_attended, grad_w_ffn = tie(grad_attended, grad_w_ffn)
    grad_heads = lax.all_to_all(grad_attended, "seq", 0, 0, tiled=True)
    grad_rows = jnp.concatenate(
        [
            dot(hidden, group_cotangent, ((0,), (0,))).astype(low),
            dot(attended, grad_branch, ((0,), (0,))).astype(low),
        ]
    )
    grad_rows = grad_rows.reshape(704, 8, 128).transpose(1, 0, 2)
    grad_rows = lax.all_to_all(grad_rows, "seq", 0, 0, tiled=True)
    block_out = (residual + multiply_scatter(hidden, weight_down, False)).astype(low)[None]

    ffn_sums = grad_w_ffn.astype(wide).sum(0).reshape(2, 64, 1152)
    ffn_send = jnp.where(half == 0, ffn_sums[1], ffn_sums[0]).astype(low)
    ffn_sums = jnp.where(half == 0, ffn_sums[0], ffn_sums[1]) + lax.ppermute(
        ffn_send, "shard", HALF_SWAP
    ).astype(wide)
    ffn_shares = lax.all_to_all(
        ffn_sums.astype(low), "shard", 0, 0, axis_index_groups=GROUPS, tiled=True
    )

    back = attend_back(heads, grad_heads, log_totals)
    back, ffn_shares, grad_rows, block_out = tie(back, ffn_shares, grad_rows, block_out)
    back = lax.all_to_all(back, "seq", 0, 0, tiled=True)

    row_sums = grad_rows.astype(wide).sum(0)
    down_sums, out_sums = row_sums[:576].reshape(2, 288, 128), row_sums[576:].reshape(2, 64, 128)
    out_keep = jnp.where(core == 0, out_sums[0], out_sums[1])
    out_arrived = swap_cores(
        jnp.where(core == 0, out_sums[1], out_sums[0]).astype(low)
    ).astype(wide)
    first = jnp.where(core == 0, out_keep, out_arrived)
    second = jnp.where(core == 0, out_arrived, out_keep)
    first, second = (
        jnp.concatenate([down_sums[0], first]),
        jnp.concatenate([down_sums[1], second]),
    )
    rows_arrived = lax.ppermute(
        jnp.where(half == 0, second, first).astype(low), "shard", HALF_SWAP
    )
    row_shares = (jnp.where(half == 0, first, second) + rows_arrived.astype(wide)).astype(low)
    down_share = row_shares[:288].reshape(9, 32, 128).transpose(1, 0, 2).reshape(32, 1152)
    out_share = row_shares[288:].reshape(8, 8, 128).transpose(1, 0, 2).reshape(8, 1024)
    _, rope_pull = jax.vjp(rope_local, query_raw, key_raw, q_scale, k_scale)
    grad_query_raw, grad_key_raw, grad_q_gain, grad_k_gain = rope_pull(
        (back[:, :128].astype(wide), back[:, 128:192].astype(wide))
    )
    grad_raw = jnp.concatenate(
        [grad_query_raw.astype(low), grad_key_raw.astype(low), back[:, 192:]], axis=1
    )
    grad_w_qkv = dot(normed, grad_raw, ((0,), (0,))).astype(low)
    grad_attn_gain = (dot(grad_raw, weight_qkv, ((1,), (1,))) * scaled).sum(0)

    grad_gains = jnp.concatenate(
        [
            grad_attn_gain.reshape(16, 64),
            grad_ffn_gain.reshape(16, 64),
            grad_q_gain.reshape(16, 4),
            grad_k_gain.reshape(16, 4),
        ],
        axis=1,
    ).astype(low)
    grad_gains = jnp.pad(grad_gains, ((0, 0), (0, 1024 - 136))).reshape(16, 8, 128)
    grad_columns = jnp.concatenate(
        [
            grad_w_qkv.reshape(16, 8, 8, 256).transpose(1, 0, 2, 3),
            jnp.broadcast_to(grad_gains[None], (8, 16, 8, 128)),
        ],
        axis=3,
    ).reshape(128, 8, 384)
    grad_columns = lax.all_to_all(grad_columns, ("seq", "shard"), 0, 0, tiled=True)
    grad_columns = grad_columns.reshape(16, 8, 8, 384)
    grad_columns = grad_columns.astype(wide).sum(0)
    gain_sums = grad_columns[:, :, 256:].sum(0).reshape(-1)
    head_shares = grad_columns[:, :, :256].astype(low)
    head_shares = head_shares.reshape(4, 16, 256).transpose(1, 0, 2).reshape(16, 1024)
    shares = jnp.concatenate(
        [
            ffn_shares.reshape(64, 1152),
            down_share,
            jnp.pad(jnp.concatenate([out_share, head_shares]), ((0, 0), (0, 128))),
        ]
    )
    shares = lax.all_to_all(
        jnp.broadcast_to(shares[None], (8,) + shares.shape), "seq", 0, 0, tiled=True
    )

    grad_normed = multiply_scatter(grad_raw, weight_qkv, True)
    _, attn_pull = jax.vjp(lambda values: rms_norm(values, attn_scale), inputs)
    (grad_inputs,) = attn_pull(grad_normed)
    grad_tokens = (grad_inputs + grad_residual).astype(low)[None]

    grad_w_gate, grad_w_up, grad_w_down, grad_w_out, grad_w_query, grad_w_key, grad_w_value = call(
        unpack_kernel,
        tuple(
            jax.ShapeDtypeStruct(shape, wide)
            for shape in (
                (64, 4608),
                (64, 4608),
                (288, width),
                (64, width),
                (64, width),
                (64, 512),
                (64, 512),
            )
        ),
        shares,
    )
    return (
        block_out,
        grad_tokens,
        gain_sums[:64],
        grad_w_query,
        grad_w_key,
        grad_w_value,
        gain_sums[128:132],
        gain_sums[132:136],
        grad_w_out,
        gain_sums[64:128],
        grad_w_gate,
        grad_w_up,
        grad_w_down,
    )


def solution(mesh):
    placed = (
        P("shard", "seq", None),
        P("shard"),
        P("shard", None),
        P("shard", None),
        P("shard", None),
        P("shard"),
        P("shard"),
        P("shard", None),
        P("shard"),
        P("shard", None),
        P("shard", None),
        P("shard", None),
        P("shard", "seq", None),
    )
    return jax.shard_map(
        per_device,
        mesh=mesh,
        in_specs=placed,
        out_specs=(
            P("shard", "seq", None),
            P("shard", "seq", None),
            P("shard"),
            P("shard", None),
            P("shard", None),
            P("shard", None),
            P("shard"),
            P("shard"),
            P("shard", None),
            P("shard"),
            P("shard", None),
            P("shard", None),
            P("shard", None),
        ),
        check_vma=False,
    )
```
